32 devices in a mesh: groups: 2 (over y), dp: 4 (over x, core), tensor: 4 (over z).
Axes of the slice: x: 2, y: 2, z: 4, core: 2. Of those that a mesh axis runs over, the one named last changes fastest.
Arguments:
- query_inputs: bfloat16 [4096, 5120], P('dp', 'tensor'), may hold values from -6 to 6
- query_grads: bfloat16 [4096, 13824], P('dp', 'tensor'), may hold values from -1.09375 to 1.09375
- input_factor: bfloat16 [64, 5120], P(None, 'tensor'), may hold values from -0.078125 to 0.078125
- output_factor: bfloat16 [64, 13824], P(None, 'tensor'), may hold values from -0.0546875 to 0.0546875
- train_store: bfloat16 [8192, 4096], P(('groups', 'dp', 'tensor')), parts along dimension 0, may hold values from -0.09375 to 0.09375
Outputs:
- scores: float32 [8192, 128], P(('groups', 'dp', 'tensor')), parts along dimension 0
The draws below stay inside these ranges and needn't reach their ends.
There are 2 independent parts, one for each index of `groups`. The reference program is written for one: setup_inputs(seed, part) draws one part's arguments, and reference() takes and returns one part's arrays. A program takes and returns all parts, laid end to end along the dimension named above; an argument that names none is the same for every part. Nothing has to cross between parts.
All inputs are finite; a program needn't handle non-finite values.
Results may differ from the reference program's by a relative error of at most 0.0029.
Values may be sent and summed in bfloat16 or wider, within the bound.
A program may use at most 64 MiB of HBM per device.

```python
import jax
import jax.numpy as jnp
from jax import lax

D = 5120
FF = 13824
K = 64
SEQ = 32
QTOK = 4096
NTR = 4096


def block_levels(rng, dims, cuts, low, high):
    def one(position, shards_of):
        draws = jax.random.uniform(jax.random.fold_in(jax.random.fold_in(rng, 6), position), (shards_of,), jnp.float32, low / len(cuts), high / len(cuts))
        return jnp.repeat(jnp.exp(draws), dims[position] // shards_of).reshape((-1,) + (1,) * (len(dims) - position - 1))

    factor_of = one(*cuts[0])
    for cut in cuts[1:]:
        factor_of = factor_of * one(*cut)
    return factor_of


def noise(stream_key, dims, scale, most, split=(), dtype=jnp.bfloat16):
    loudness = block_levels(stream_key, dims, split, -0.22, 0.18) if split else 1.0
    values = jax.random.normal(stream_key, dims, jnp.float32) * scale * loudness
    return jnp.minimum(jnp.maximum(values, -most), most).astype(dtype)


def setup_inputs(seed: int = 0, part: int = 0) -> dict:
    streams_of = jax.random.split(jax.random.key(seed), 6)
    part_keys = jax.random.split(jax.random.fold_in(streams_of[5], part), 6)
    return {
        "query_inputs": noise(streams_of[0], (QTOK, D), 1.0, 6.0, ((0, 4), (1, 4))),
        "query_grads": noise(streams_of[1], (QTOK, FF), 0.18, 1.09375, ((0, 4), (1, 4))),
        "input_factor": noise(streams_of[2], (K, D), D ** -0.5, 0.078125, ((1, 4),)),
        "output_factor": noise(streams_of[3], (K, FF), FF ** -0.5, 0.0546875, ((1, 4),)),
        "train_store": noise(part_keys[4], (NTR, K * K), (K * K) ** -0.5, 0.09375, ((0, 16),)),
    }


def reference(query_inputs, query_grads, input_factor, output_factor, train_store):
    inputs_projected = jnp.dot(query_inputs, input_factor.T, preferred_element_type=jnp.float32)
    grads_projected = jnp.dot(query_grads, output_factor.T, preferred_element_type=jnp.float32)
    examples = inputs_projected.shape[0] // SEQ
    query_gradient = jnp.einsum(
        "eto,eti->eoi",
        grads_projected.reshape(examples, SEQ, K),
        inputs_projected.reshape(examples, SEQ, K),
        precision=lax.Precision.HIGHEST,
    ).reshape(examples, K * K).astype(jnp.bfloat16)
    return jnp.dot(train_store, query_gradient.T, preferred_element_type=jnp.float32)
```

```python
import jax
import jax.numpy as jnp
from jax import lax
from jax.experimental import pallas as pl
from jax.experimental.pallas import tpu as pltpu
from jax.sharding import PartitionSpec as P

K = 64
SEQ = 32
HIGHEST = lax.Precision.HIGHEST


def dot_rows(a, b):
    return lax.dot_general(a, b, (((1,), (1,)), ((), ())), preferred_element_type=jnp.float32)


def fused_kernel(
    qi_hbm, qg_hbm, fi_hbm, fo_hbm, store_hbm, out_ref,
    qi, qg, fi, fo, store, part, got, turned, spread, blocks, wide,
    load_sem, rs_send, rs_recv, ag_send, ag_recv,
):
    depth = lax.axis_size("tensor")
    rows = qi.shape[1]
    y = lax.axis_index("groups")
    dp = lax.axis_index("dp")
    z = lax.axis_index("tensor")
    x = dp // 2
    core = dp % 2
    other_core = {"dp": x * 2 + (1 - core)}
    other_x = {"dp": (1 - x) * 2 + core}
    other_y = {"groups": 1 - y}
    order = (2, 1, 3, 0)

    def load(source, target, index):
        return pltpu.make_async_copy(source, target, load_sem.at[index])

    def chunk_loads(step):
        target = lax.rem(z + step, depth)
        start = pl.multiple_of((y * depth + target) * rows, rows)
        return (
            load(qi_hbm.at[pl.ds(start, rows), :], qi.at[step], 3 + 2 * step),
            load(qg_hbm.at[pl.ds(start, rows), :], qg.at[step], 4 + 2 * step),
        )

    load(fi_hbm, fi, 0).start()
    load(fo_hbm, fo, 1).start()
    for step in order:
        for copy in chunk_loads(step):
            copy.start()
    load(store_hbm, store, 2).start()

    barrier = pltpu.get_barrier_semaphore()
    partners = [{"tensor": lax.rem(z + step, depth)} for step in range(1, 4)]
    partners += [other_core, other_x, other_y]
    for partner in partners:
        pl.semaphore_signal(barrier, inc=1, device_id=partner, device_id_type=pl.DeviceIdType.MESH)

    def remote(source, target, send, recv, device):
        return pltpu.make_async_remote_copy(
            src_ref=source, dst_ref=target, send_sem=send, recv_sem=recv,
            device_id=device, device_id_type=pl.DeviceIdType.MESH,
        )

    def rs_copy(step):
        device = {"tensor": lax.rem(z + step, depth)}
        slot = step - 1
        return remote(part.at[slot], got.at[slot], rs_send.at[slot], rs_recv.at[slot], device)

    load(fi_hbm, fi, 0).wait()
    load(fo_hbm, fo, 1).wait()
    total = None
    for step in order:
        for copy in chunk_loads(step):
            copy.wait()
        summed = jnp.concatenate([dot_rows(qi[step], fi[...]), dot_rows(qg[step], fo[...])], axis=1)
        if step == 0:
            total = summed
            continue
        part[step - 1] = summed
        if step == order[0]:
            pl.semaphore_wait(barrier, len(partners))
        rs_copy(step).start()

    for step in (1, 2, 3):
        rs_copy(step).wait_recv()
        total = total + got[step - 1]

    turned[...] = total.T
    token = lax.broadcasted_iota(jnp.int32, (K // 2, rows), 1) // SEQ
    for half in range(2):
        picked = turned[pl.ds(K + half, K // 2, stride=2), :]
        for q in range(4):
            spread[half, pl.ds(q, K // 2, stride=4), :] = jnp.where(token == q, picked, 0.0)
    lane = lax.broadcasted_iota(jnp.int32, total.shape, 1)
    stacked = jnp.concatenate(
        [jnp.where(lane < K, total, 0.0), jnp.where(lane >= K, pltpu.roll(total, K, 1), 0.0)], axis=0
    )
    gradient = jnp.dot(jnp.concatenate([spread[0], spread[1]], axis=1), stacked, precision=HIGHEST, preferred_element_type=jnp.float32)

    def slot_of(yy, xx, zz, cc):
        return ((xx * 2 + cc) * 2 + yy) * depth + zz

    blocks[slot_of(y, x, z, core)] = gradient.astype(jnp.bfloat16)

    def move(slot, kind, zz, device):
        return remote(blocks.at[slot], blocks.at[slot], ag_send.at[kind, zz], ag_recv.at[slot], device)

    def arrived(slot):
        remote(blocks.at[slot], blocks.at[slot], ag_send.at[0, 0], ag_recv.at[slot], other_core).wait_recv()

    def column(zz, up, down):
        slot = slot_of(y, x, zz, core)

        @pl.when(jnp.logical_and(up, z < depth - 1))
        def _():
            move(slot, 0, zz, {"tensor": jnp.minimum(z + 1, depth - 1)}).start()

        @pl.when(jnp.logical_and(down, z > 0))
        def _():
            move(slot, 1, zz, {"tensor": jnp.maximum(z - 1, 0)}).start()

        move(slot, 2, zz, other_x).start()
        move(slot, 3, zz, other_y).start()
        move(slot, 4, zz, other_core).start()

    def neighbours(zz):
        along_x = slot_of(y, 1 - x, zz, core)
        along_y = slot_of(1 - y, x, zz, core)
        even = zz % 2 == 0
        arrived(along_x)

        @pl.when(even)
        def _():
            move(along_x, 8, zz, other_y).start()

        move(along_x, 5, zz, other_core).start()
        arrived(along_y)

        @pl.when(jnp.logical_not(even))
        def _():
            move(along_y, 8, zz, other_x).start()

        move(along_y, 6, zz, other_core).start()

    def at_distance(step, act):
        if step == 0:
            act(z, True, True)
            return

        @pl.when(z - step >= 0)
        def _():
            act(jnp.maximum(z - step, 0), True, False)

        @pl.when(z + step < depth)
        def _():
            act(jnp.minimum(z + step, depth - 1), False, True)

    def arrived_column(zz, up, down):
        arrived(slot_of(y, x, zz, core))
        column(zz, up, down)

    low = lax.broadcasted_iota(jnp.int32, (16, 8, 128), 1) < 4

    def regroup(yy, xx, cc):
        base = slot_of(yy, xx, 0, cc)
        evens, odds = [], []
        for pair in range(2):
            a = blocks[base + 2 * pair].astype(jnp.float32).reshape(16, 8, 128)
            b = blocks[base + 2 * pair + 1].astype(jnp.float32).reshape(16, 8, 128)
            evens.append(jnp.where(low, a, pltpu.roll(b, 4, 1)))
            odds.append(jnp.where(low, pltpu.roll(a, 4, 1), b))
        even = jnp.concatenate(evens, axis=1).astype(jnp.bfloat16)
        odd = jnp.concatenate(odds, axis=1).astype(jnp.bfloat16)
        start = pl.multiple_of(base * 4, 16)
        for m in range(16):
            wide[pl.ds(start, 16), m * 256 : m * 256 + 128] = even[m]
            wide[pl.ds(start, 16), m * 256 + 128 : (m + 1) * 256] = odd[m]

    column(z, True, True)
    for step in range(1, 4):
        at_distance(step, arrived_column)
        at_distance(step - 1, lambda zz, up, down: neighbours(zz))
    at_distance(3, lambda zz, up, down: neighbours(zz))
    regroup(y, x, core)
    regroup(y, 1 - x, core)
    regroup(1 - y, x, core)
    for zz in range(4):
        slot = slot_of(1 - y, 1 - x, zz, core)
        arrived(slot)
        move(slot, 7, zz, other_core).start()
    regroup(1 - y, 1 - x, core)
    for yy, xx in ((y, x), (y, 1 - x), (1 - y, x), (1 - y, 1 - x)):
        for zz in range(4):
            arrived(slot_of(yy, xx, zz, 1 - core))
        regroup(yy, xx, 1 - core)

    load(store_hbm, store, 2).wait()
    out_ref[...] = dot_rows(store[...], wide[...])

    for step in (1, 2, 3):
        rs_copy(step).wait_send()
    own = slot_of(y, x, z, core)

    def sent(kind, zz):
        move(own, kind, zz, other_core).wait_send()

    for zz in range(4):
        for kind in range(2, 9):
            sent(kind, zz)

        @pl.when(jnp.logical_and(zz <= z, z < depth - 1))
        def _():
            sent(0, zz)

        @pl.when(jnp.logical_and(zz >= z, z > 0))
        def _():
            sent(1, zz)


def fused(query_inputs, query_grads, input_factor, output_factor, train_store):
    tokens, width = query_inputs.shape
    hidden = query_grads.shape[1]
    rows = tokens // 8
    queries = 32 * 4
    any_spec = pl.BlockSpec(memory_space=pl.ANY)
    return pl.pallas_call(
        fused_kernel,
        out_shape=jax.ShapeDtypeStruct((train_store.shape[0], queries), jnp.float32),
        in_specs=[any_spec] * 5,
        out_specs=pl.BlockSpec(memory_space=pltpu.VMEM),
        scratch_shapes=[
            pltpu.VMEM((4, rows, width), jnp.bfloat16),
            pltpu.VMEM((4, rows, hidden), jnp.bfloat16),
            pltpu.VMEM(input_factor.shape, jnp.bfloat16),
            pltpu.VMEM(output_factor.shape, jnp.bfloat16),
            pltpu.VMEM(train_store.shape, jnp.bfloat16),
            pltpu.VMEM((3, rows, 2 * K), jnp.float32),
            pltpu.VMEM((3, rows, 2 * K), jnp.float32),
            pltpu.VMEM((2 * K, rows), jnp.float32),
            pltpu.VMEM((2, rows, rows), jnp.float32),
            pltpu.VMEM((32, rows, 2 * K), jnp.bfloat16),
            pltpu.VMEM((queries, K * K), jnp.bfloat16),
            pltpu.SemaphoreType.DMA((11,)),
            pltpu.SemaphoreType.DMA((3,)),
            pltpu.SemaphoreType.DMA((3,)),
            pltpu.SemaphoreType.DMA((9, 4)),
            pltpu.SemaphoreType.DMA((32,)),
        ],
        compiler_params=pltpu.CompilerParams(
            collective_id=0, has_side_effects=True, vmem_limit_bytes=40 * 1024 * 1024
        ),
        cost_estimate=pl.CostEstimate(flops=1_000_000_000, bytes_accessed=8_000_000, transcendentals=0),
    )(query_inputs, query_grads, input_factor, output_factor, train_store)


def from_behind(value, axis, steps):
    count = lax.axis_size(axis)
    pairs = [(source, (source + steps) % count) for source in range(count)]
    return lax.ppermute(value, axis, pairs)


def outer_blocks(inputs_rows, grads_rows):
    examples = inputs_rows.shape[0] // SEQ
    blocks = jnp.einsum(
        "eto,eti->eoi",
        grads_rows.reshape(examples, SEQ, K),
        inputs_rows.reshape(examples, SEQ, K),
        precision=HIGHEST,
    )
    return blocks.reshape(examples, K * K).astype(jnp.bfloat16)


def ring(query_inputs, query_grads, input_factor, output_factor, train_store):
    inputs_part = dot_rows(query_inputs, input_factor)
    grads_part = dot_rows(query_grads, output_factor)
    inputs_full, grads_full = lax.psum((inputs_part, grads_part), "tensor")
    block = outer_blocks(inputs_full, grads_full)

    def place_block(scores, piece, start):
        return lax.dynamic_update_slice_in_dim(scores, dot_rows(train_store, piece), start, 1)

    per_owner = block.shape[0]
    cycle_size = lax.axis_size("dp")
    own_index = lax.axis_index("dp")
    scores_empty = jnp.zeros((train_store.shape[0], per_owner * cycle_size), jnp.float32)
    scores = place_block(scores_empty, block, own_index * per_owner)

    def cycle_step(turn, carry):
        held, scores = carry
        held = from_behind(held, "dp", 1)
        owner = (own_index - turn) % cycle_size
        return (held, place_block(scores, held, owner * per_owner))

    held, scores = lax.fori_loop(1, cycle_size, cycle_step, (block, scores))
    return scores


def local(query_inputs, *rest):
    sizes = tuple(lax.axis_size(axis) for axis in ("groups", "dp", "tensor"))
    if sizes == (2, 4, 4) and query_inputs.shape[0] == 8 * 4 * SEQ:
        return fused(query_inputs, *rest)
    return ring(query_inputs, *rest)


def solution(mesh):
    return jax.shard_map(
        local,
        mesh=mesh,
        in_specs=(
            P("dp", "tensor"),
            P("dp", "tensor"),
            P(None, "tensor"),
            P(None, "tensor"),
            P(("groups", "dp", "tensor"), None),
        ),
        out_specs=P(("groups", "dp", "tensor"), None),
        check_vma=False,
    )
```

```python
import jax
import jax.numpy as jnp
from jax import lax
from jax.experimental import pallas as pl
from jax.experimental.pallas import tpu as pltpu
from jax.sharding import PartitionSpec as P

K = 64
SEQ = 32
HIGHEST = lax.Precision.HIGHEST


def dot_rows(a, b):
    return lax.dot_general(a, b, (((1,), (1,)), ((), ())), preferred_element_type=jnp.float32)


def fused_kernel(
    qi_hbm, qg_hbm, fi_hbm, fo_hbm, store_hbm, out_ref,
    qi, qg, fi, fo, store, part, got, turned, spread, blocks, wide,
    load_sem, rs_send, rs_recv, ag_send, ag_recv,
):
    depth = lax.axis_size("tensor")
    rows = qi.shape[1]
    y = lax.axis_index("groups")
    dp = lax.axis_index("dp")
    z = lax.axis_index("tensor")
    x = dp // 2
    core = dp % 2
    other_core = {"dp": x * 2 + (1 - core)}
    other_x = {"dp": (1 - x) * 2 + core}
    other_y = {"groups": 1 - y}
    other_xy = {"groups": 1 - y, "dp": (1 - x) * 2 + core}
    order = (2, 3, 1, 0)

    def peer(step):
        return (z, z + 1 - 2 * (z % 2), lax.rem(z + 2, depth), depth - 1 - z)[step]

    def load(source, target, index):
        return pltpu.make_async_copy(source, target, load_sem.at[index])

    def chunk_loads(step):
        start = pl.multiple_of((y * depth + peer(step)) * rows, rows)
        return (
            load(qi_hbm.at[pl.ds(start, rows), :], qi.at[step], 3 + 2 * step),
            load(qg_hbm.at[pl.ds(start, rows), :], qg.at[step], 4 + 2 * step),
        )

    load(fi_hbm, fi, 0).start()
    load(fo_hbm, fo, 1).start()
    for step in order:
        for copy in chunk_loads(step):
            copy.start()
    load(store_hbm, store, 2).start()

    barrier = pltpu.get_barrier_semaphore()
    partners = [{"tensor": peer(step)} for step in range(1, 4)]
    partners += [other_core, other_x, other_y, other_xy]
    for partner in partners:
        pl.semaphore_signal(barrier, inc=1, device_id=partner, device_id_type=pl.DeviceIdType.MESH)

    def remote(source, target, send, recv, device):
        return pltpu.make_async_remote_copy(
            src_ref=source, dst_ref=target, send_sem=send, recv_sem=recv,
            device_id=device, device_id_type=pl.DeviceIdType.MESH,
        )

    def rs_copy(step):
        device = {"tensor": peer(step)}
        slot = step - 1
        return remote(part.at[slot], got.at[slot], rs_send.at[slot], rs_recv.at[slot], device)

    load(fi_hbm, fi, 0).wait()
    load(fo_hbm, fo, 1).wait()
    total = None
    for step in order:
        for copy in chunk_loads(step):
            copy.wait()
        summed = jnp.concatenate([dot_rows(qi[step], fi[...]), dot_rows(qg[step], fo[...])], axis=1)
        if step == 0:
            total = summed
            continue
        part[step - 1] = summed
        if step == order[0]:
            pl.semaphore_wait(barrier, len(partners))
        rs_copy(step).start()

    for step in (1, 2, 3):
        rs_copy(step).wait_recv()
        total = total + got[step - 1]

    turned[...] = total.T
    token = lax.broadcasted_iota(jnp.int32, (K // 2, rows), 1) // SEQ
    for half in range(2):
        picked = turned[pl.ds(K + half, K // 2, stride=2), :]
        for q in range(4):
            spread[half, pl.ds(q, K // 2, stride=4), :] = jnp.where(token == q, picked, 0.0)
    lane = lax.broadcasted_iota(jnp.int32, total.shape, 1)
    stacked = jnp.concatenate(
        [jnp.where(lane < K, total, 0.0), jnp.where(lane >= K, pltpu.roll(total, K, 1), 0.0)], axis=0
    )
    gradient = jnp.dot(jnp.concatenate([spread[0], spread[1]], axis=1), stacked, precision=HIGHEST, preferred_element_type=jnp.float32)

    def slot_of(yy, xx, zz, cc):
        return ((xx * 2 + cc) * 2 + yy) * depth + zz

    blocks[slot_of(y, x, z, core)] = gradient.astype(jnp.bfloat16)

    def move(slot, kind, zz, device):
        return remote(blocks.at[slot], blocks.at[slot], ag_send.at[kind, zz], ag_recv.at[slot], device)

    def arrived(slot):
        remote(blocks.at[slot], blocks.at[slot], ag_send.at[0, 0], ag_recv.at[slot], other_core).wait_recv()

    def column(step):
        zz = peer(step)
        slot = slot_of(y, x, zz, core)
        if step:
            arrived(slot)
        for kind, device in enumerate((other_xy, other_x, other_y, other_core)):
            move(slot, kind, zz, device).start()

    def plane(step):
        zz = peer(step)
        for kind, (yy, xx) in enumerate(((y, 1 - x), (1 - y, x), (1 - y, 1 - x))):
            slot = slot_of(yy, xx, zz, core)
            arrived(slot)
            move(slot, 4 + kind, zz, other_core).start()

    low = lax.broadcasted_iota(jnp.int32, (16, 8, 128), 1) < 4

    def regroup(yy, xx, cc):
        base = slot_of(yy, xx, 0, cc)
        evens, odds = [], []
        for pair in range(2):
            a = blocks[base + 2 * pair].astype(jnp.float32).reshape(16, 8, 128)
            b = blocks[base + 2 * pair + 1].astype(jnp.float32).reshape(16, 8, 128)
            evens.append(jnp.where(low, a, pltpu.roll(b, 4, 1)))
            odds.append(jnp.where(low, pltpu.roll(a, 4, 1), b))
        even = jnp.concatenate(evens, axis=1).astype(jnp.bfloat16)
        odd = jnp.concatenate(odds, axis=1).astype(jnp.bfloat16)
        start = pl.multiple_of(base * 4, 16)
        for m in range(16):
            wide[pl.ds(start, 16), m * 256 : m * 256 + 128] = even[m]
            wide[pl.ds(start, 16), m * 256 + 128 : (m + 1) * 256] = odd[m]

    for step in (2, 3, 1):
        move(slot_of(y, x, z, core), 6 + step, z, {"tensor": peer(step)}).start()
    for step in (0, 1, 3, 2):
        column(step)
    regroup(y, x, core)
    for step in (0, 1, 3, 2):
        plane(step)
    regroup(y, 1 - x, core)
    regroup(1 - y, x, core)
    regroup(1 - y, 1 - x, core)
    for yy, xx in ((y, x), (y, 1 - x), (1 - y, x), (1 - y, 1 - x)):
        for zz in range(4):
            arrived(slot_of(yy, xx, zz, 1 - core))
        regroup(yy, xx, 1 - core)

    load(store_hbm, store, 2).wait()
    out_ref[...] = dot_rows(store[...], wide[...])

    for step in (1, 2, 3):
        rs_copy(step).wait_send()
    own = slot_of(y, x, z, core)

    for zz in range(4):
        for kind in range(7):
            move(own, kind, zz, other_core).wait_send()
    for step in (1, 2, 3):
        move(own, 6 + step, z, other_core).wait_send()


def fused(query_inputs, query_grads, input_factor, output_factor, train_store):
    tokens, width = query_inputs.shape
    hidden = query_grads.shape[1]
    rows = tokens // 8
    queries = 32 * 4
    any_spec = pl.BlockSpec(memory_space=pl.ANY)
    return pl.pallas_call(
        fused_kernel,
        out_shape=jax.ShapeDtypeStruct((train_store.shape[0], queries), jnp.float32),
        in_specs=[any_spec] * 5,
        out_specs=pl.BlockSpec(memory_space=pltpu.VMEM),
        scratch_shapes=[
            pltpu.VMEM((4, rows, width), jnp.bfloat16),
            pltpu.VMEM((4, rows, hidden), jnp.bfloat16),
            pltpu.VMEM(input_factor.shape, jnp.bfloat16),
            pltpu.VMEM(output_factor.shape, jnp.bfloat16),
            pltpu.VMEM(train_store.shape, jnp.bfloat16),
            pltpu.VMEM((3, rows, 2 * K), jnp.float32),
            pltpu.VMEM((3, rows, 2 * K), jnp.float32),
            pltpu.VMEM((2 * K, rows), jnp.float32),
            pltpu.VMEM((2, rows, rows), jnp.float32),
            pltpu.VMEM((32, rows, 2 * K), jnp.bfloat16),
            pltpu.VMEM((queries, K * K), jnp.bfloat16),
            pltpu.SemaphoreType.DMA((11,)),
            pltpu.SemaphoreType.DMA((3,)),
            pltpu.SemaphoreType.DMA((3,)),
            pltpu.SemaphoreType.DMA((10, 4)),
            pltpu.SemaphoreType.DMA((32,)),
        ],
        compiler_params=pltpu.CompilerParams(
            collective_id=0, has_side_effects=True, vmem_limit_bytes=60 * 1024 * 1024
        ),
        cost_estimate=pl.CostEstimate(flops=1_000_000_000, bytes_accessed=8_000_000, transcendentals=0),
    )(query_inputs, query_grads, input_factor, output_factor, train_store)


def from_behind(value, axis, steps):
    count = lax.axis_size(axis)
    pairs = [(source, (source + steps) % count) for source in range(count)]
    return lax.ppermute(value, axis, pairs)


def outer_blocks(inputs_rows, grads_rows):
    examples = inputs_rows.shape[0] // SEQ
    blocks = jnp.einsum(
        "eto,eti->eoi",
        grads_rows.reshape(examples, SEQ, K),
        inputs_rows.reshape(examples, SEQ, K),
        precision=HIGHEST,
    )
    return blocks.reshape(examples, K * K).astype(jnp.bfloat16)


def ring(query_inputs, query_grads, input_factor, output_factor, train_store):
    inputs_part = dot_rows(query_inputs, input_factor)
    grads_part = dot_rows(query_grads, output_factor)
    inputs_full, grads_full = lax.psum((inputs_part, grads_part), "tensor")
    block = outer_blocks(inputs_full, grads_full)

    def place_block(scores, piece, start):
        return lax.dynamic_update_slice_in_dim(scores, dot_rows(train_store, piece), start, 1)

    per_owner = block.shape[0]
    cycle_size = lax.axis_size("dp")
    own_index = lax.axis_index("dp")
    scores_empty = jnp.zeros((train_store.shape[0], per_owner * cycle_size), jnp.float32)
    scores = place_block(scores_empty, block, own_index * per_owner)

    def cycle_step(turn, carry):
        held, scores = carry
        held = from_behind(held, "dp", 1)
        owner = (own_index - turn) % cycle_size
        return (held, place_block(scores, held, owner * per_owner))

    held, scores = lax.fori_loop(1, cycle_size, cycle_step, (block, scores))
    return scores


def local(query_inputs, *rest):
    sizes = tuple(lax.axis_size(axis) for axis in ("groups", "dp", "tensor"))
    if sizes == (2, 4, 4) and query_inputs.shape[0] == 8 * 4 * SEQ:
        return fused(query_inputs, *rest)
    return ring(query_inputs, *rest)


def solution(mesh):
    return jax.shard_map(
        local,
        mesh=mesh,
        in_specs=(
            P("dp", "tensor"),
            P("dp", "tensor"),
            P(None, "tensor"),
            P(None, "tensor"),
            P(("groups", "dp", "tensor"), None),
        ),
        out_specs=P(("groups", "dp", "tensor"), None),
        check_vma=False,
    )
```

```python
import jax
import jax.numpy as jnp
from jax import lax
from jax.experimental import pallas as pl
from jax.experimental.pallas import tpu as pltpu
from jax.sharding import PartitionSpec as P

K = 64
SEQ = 32
HIGHEST = lax.Precision.HIGHEST


def dot_rows(a, b):
    return lax.dot_general(a, b, (((1,), (1,)), ((), ())), preferred_element_type=jnp.float32)


def fused_kernel(
    qi_hbm, qg_hbm, fi_hbm, fo_hbm, store_hbm, out_ref,
    qi, qg, fi, fo, store, part, got, turned, spread, blocks, wide,
    load_sem, rs_send, rs_recv, ag_send, ag_recv, group_recv,
):
    depth = lax.axis_size("tensor")
    rows = qi.shape[1]
    y = lax.axis_index("groups")
    dp = lax.axis_index("dp")
    z = lax.axis_index("tensor")
    x = dp // 2
    core = dp % 2
    other_core = {"dp": x * 2 + (1 - core)}
    other_x = {"dp": (1 - x) * 2 + core}
    other_y = {"groups": 1 - y}
    other_xy = {"groups": 1 - y, "dp": (1 - x) * 2 + core}
    order = (3, 2, 1, 0)
    half = rows // 2

    def peer(step):
        return (z, z + 1 - 2 * (z % 2), lax.rem(z + 2, depth), depth - 1 - z)[step]

    def load(source, target, index):
        return pltpu.make_async_copy(source, target, load_sem.at[index])

    def chunk_loads(step):
        start = pl.multiple_of((y * depth + peer(step)) * rows, rows)
        return (
            load(qi_hbm.at[pl.ds(start, rows), :], qi.at[step], 3 + 2 * step),
            load(qg_hbm.at[pl.ds(start, rows), :], qg.at[step], 4 + 2 * step),
        )

    load(fi_hbm, fi, 0).start()
    load(fo_hbm, fo, 1).start()
    for step in order:
        for copy in chunk_loads(step):
            copy.start()
    load(store_hbm, store, 2).start()

    barrier = pltpu.get_barrier_semaphore()
    partners = [{"tensor": peer(step)} for step in range(1, 4)]
    partners += [other_core, other_x, other_y, other_xy]
    for partner in partners:
        pl.semaphore_signal(barrier, inc=1, device_id=partner, device_id_type=pl.DeviceIdType.MESH)

    def remote(source, target, send, recv, device):
        return pltpu.make_async_remote_copy(
            src_ref=source, dst_ref=target, send_sem=send, recv_sem=recv,
            device_id=device, device_id_type=pl.DeviceIdType.MESH,
        )

    def sums(kind):
        source, step = (
            (part.at[3, pl.ds(half, half)], 1),
            (part.at[3, pl.ds(0, half)], 3),
            (part.at[2, pl.ds(0, half)], 2),
            (part.at[1, pl.ds(0, half)], 1),
            (part.at[1, pl.ds(half, half)], 1),
            (part.at[2, pl.ds(half, half)], 2),
        )[kind]
        return remote(source, got.at[kind], rs_send.at[kind], rs_recv.at[kind], {"tensor": peer(step)})

    load(fi_hbm, fi, 0).wait()
    load(fo_hbm, fo, 1).wait()
    for step in order:
        for copy in chunk_loads(step):
            copy.wait()
        part[step] = jnp.concatenate([dot_rows(qi[step], fi[...]), dot_rows(qg[step], fo[...])], axis=1)
        if step == order[0]:
            pl.semaphore_wait(barrier, len(partners))
        for kind in ((), (3, 4), (2,), (0, 1))[step]:
            sums(kind).start()

    sums(0).wait_recv()
    part[2, half:] = part[2, half:] + got[0]
    sums(5).start()

    lane = lax.broadcasted_iota(jnp.int32, (half, 2 * K), 1)
    lane8 = lax.broadcasted_iota(jnp.int32, (8, 2 * half), 1)

    def query_gradients(total):
        turned[...] = jnp.concatenate([total, total], axis=0).T
        for place, pair in enumerate((0, 2, 1, 3)):
            first = turned[pl.ds(K + 2 * pair, 8, stride=8), :]
            second = turned[pl.ds(K + 2 * pair + 1, 8, stride=8), :]
            both = jnp.where(lane8 < half, first, second)
            for q in range(2):
                spread[pl.ds(place * 2 + q, 8, stride=8), :] = jnp.where((lane8 % half) // SEQ == q, both, 0.0)
        stacked = jnp.concatenate(
            [jnp.where(lane < K, total, 0.0), jnp.where(lane >= K, pltpu.roll(total, K, 1), 0.0)], axis=0
        )
        product = jnp.dot(spread[...], stacked, precision=HIGHEST, preferred_element_type=jnp.float32)
        return product.astype(jnp.bfloat16)

    def slot_of(yy, xx, zz, cc):
        return ((xx * 2 + cc) * 2 + yy) * depth + zz

    def move(part_of, slot, kind, zz, device):
        block = blocks.at[part_of * 32 + slot]
        recv = group_recv.at[part_of, slot // depth] if kind < 3 else ag_recv.at[part_of, zz]
        return remote(block, block, ag_send, recv, device)

    def four(part_of, yy, xx, cc):
        base = slot_of(yy, xx, 0, cc)
        blocks_of = blocks.at[pl.ds(part_of * 32 + base, 4)]
        return remote(blocks_of, blocks_of, ag_send, group_recv.at[part_of, base // depth], other_core)

    def column(part_of, step):
        zz = peer(step)
        slot = slot_of(y, x, zz, core)
        if step:
            move(part_of, slot, 3, zz, other_core).wait_recv()
        for kind, device in enumerate((other_xy, other_x, other_y)):
            move(part_of, slot, kind, zz, device).start()

    row8 = lax.broadcasted_iota(jnp.int32, (8, 8, 2 * K), 1)
    low = row8 < 4
    first_of_two = (row8 // 2) % 2 == 0

    def pairs(slot):
        a = blocks[slot].astype(jnp.float32).reshape(8, 8, 2 * K)
        b = blocks[32 + slot].astype(jnp.float32).reshape(8, 8, 2 * K)
        return jnp.where(first_of_two, a, pltpu.roll(b, 2, 1)), jnp.where(first_of_two, pltpu.roll(a, 6, 1), b)

    def regroup(yy, xx, cc):
        base = slot_of(yy, xx, 0, cc)
        start = pl.multiple_of(base * 4, 16)
        held = [pairs(base + zz) for zz in range(4)]
        for e in range(2):
            evens, odds = [], []
            for zz in (0, 2):
                a, b = held[zz][e], held[zz + 1][e]
                evens.append(jnp.where(low, a, pltpu.roll(b, 4, 1)))
                odds.append(jnp.where(low, pltpu.roll(a, 4, 1), b))
            even = jnp.concatenate(evens, axis=1).astype(jnp.bfloat16)
            odd = jnp.concatenate(odds, axis=1).astype(jnp.bfloat16)
            for g in range(8):
                at = (2 * g + e) * 256
                wide[pl.ds(start, 16), at : at + 128] = even[g]
                wide[pl.ds(start, 16), at + 128 : at + 256] = odd[g]

    own = slot_of(y, x, z, core)
    for part_of, kinds in ((0, (3, 1, 2)), (1, (4, 5))):
        total = part[0, part_of * half : (part_of + 1) * half]
        for kind in kinds:
            sums(kind).wait_recv()
            total = total + got[kind]
        blocks[part_of * 32 + own] = query_gradients(total)
        for step in (2, 3, 1):
            move(part_of, own, 3, z, {"tensor": peer(step)}).start()
        column(part_of, 0)

    for part_of in range(2):
        for step in (1, 3, 2):
            column(part_of, step)
        four(part_of, y, x, core).start()
    chips = ((y, x), (y, 1 - x), (1 - y, x), (1 - y, 1 - x))
    for part_of in range(2):
        for yy, xx in chips[1:]:
            four(part_of, yy, xx, core).wait_recv()
            four(part_of, yy, xx, core).start()
    for cc in (core, 1 - core):
        for yy, xx in chips:
            if cc is not core:
                for part_of in range(2):
                    four(part_of, yy, xx, cc).wait_recv()
            regroup(yy, xx, cc)

    load(store_hbm, store, 2).wait()
    out_ref[...] = dot_rows(store[...], wide[...])

    for kind in range(6):
        sums(kind).wait_send()
    every = blocks.at[pl.ds(0, 62)]
    remote(every, every, ag_send, ag_recv.at[0, z], other_core).wait_send()


def fused(query_inputs, query_grads, input_factor, output_factor, train_store):
    tokens, width = query_inputs.shape
    hidden = query_grads.shape[1]
    rows = tokens // 8
    queries = 32 * 4
    any_spec = pl.BlockSpec(memory_space=pl.ANY)
    return pl.pallas_call(
        fused_kernel,
        out_shape=jax.ShapeDtypeStruct((train_store.shape[0], queries), jnp.float32),
        in_specs=[any_spec] * 5,
        out_specs=pl.BlockSpec(memory_space=pltpu.VMEM),
        scratch_shapes=[
            pltpu.VMEM((4, rows, width), jnp.bfloat16),
            pltpu.VMEM((4, rows, hidden), jnp.bfloat16),
            pltpu.VMEM(input_factor.shape, jnp.bfloat16),
            pltpu.VMEM(output_factor.shape, jnp.bfloat16),
            pltpu.VMEM(train_store.shape, jnp.bfloat16),
            pltpu.VMEM((4, rows, 2 * K), jnp.float32),
            pltpu.VMEM((6, rows // 2, 2 * K), jnp.float32),
            pltpu.VMEM((2 * K, rows), jnp.float32),
            pltpu.VMEM((rows // 2, rows), jnp.float32),
            pltpu.VMEM((64, rows // 2, 2 * K), jnp.bfloat16),
            pltpu.VMEM((queries, K * K), jnp.bfloat16),
            pltpu.SemaphoreType.DMA((11,)),
            pltpu.SemaphoreType.DMA((6,)),
            pltpu.SemaphoreType.DMA((6,)),
            pltpu.SemaphoreType.DMA,
            pltpu.SemaphoreType.DMA((2, 4)),
            pltpu.SemaphoreType.DMA((2, 8)),
        ],
        compiler_params=pltpu.CompilerParams(
            collective_id=0, has_side_effects=True, vmem_limit_bytes=60 * 1024 * 1024
        ),
        cost_estimate=pl.CostEstimate(flops=1_000_000_000, bytes_accessed=8_000_000, transcendentals=0),
    )(query_inputs, query_grads, input_factor, output_factor, train_store)


def from_behind(value, axis, steps):
    count = lax.axis_size(axis)
    pairs = [(source, (source + steps) % count) for source in range(count)]
    return lax.ppermute(value, axis, pairs)


def outer_blocks(inputs_rows, grads_rows):
    examples = inputs_rows.shape[0] // SEQ
    blocks = jnp.einsum(
        "eto,eti->eoi",
        grads_rows.reshape(examples, SEQ, K),
        inputs_rows.reshape(examples, SEQ, K),
        precision=HIGHEST,
    )
    return blocks.reshape(examples, K * K).astype(jnp.bfloat16)


def ring(query_inputs, query_grads, input_factor, output_factor, train_store):
    inputs_part = dot_rows(query_inputs, input_factor)
    grads_part = dot_rows(query_grads, output_factor)
    inputs_full, grads_full = lax.psum((inputs_part, grads_part), "tensor")
    block = outer_blocks(inputs_full, grads_full)

    def place_block(scores, piece, start):
        return lax.dynamic_update_slice_in_dim(scores, dot_rows(train_store, piece), start, 1)

    per_owner = block.shape[0]
    cycle_size = lax.axis_size("dp")
    own_index = lax.axis_index("dp")
    scores_empty = jnp.zeros((train_store.shape[0], per_owner * cycle_size), jnp.float32)
    scores = place_block(scores_empty, block, own_index * per_owner)

    def cycle_step(turn, carry):
        held, scores = carry
        held = from_behind(held, "dp", 1)
        owner = (own_index - turn) % cycle_size
        return (held, place_block(scores, held, owner * per_owner))

    held, scores = lax.fori_loop(1, cycle_size, cycle_step, (block, scores))
    return scores


def local(query_inputs, *rest):
    sizes = tuple(lax.axis_size(axis) for axis in ("groups", "dp", "tensor"))
    if sizes == (2, 4, 4) and query_inputs.shape[0] == 8 * 4 * SEQ:
        return fused(query_inputs, *rest)
    return ring(query_inputs, *rest)


def solution(mesh):
    return jax.shard_map(
        local,
        mesh=mesh,
        in_specs=(
            P("dp", "tensor"),
            P("dp", "tensor"),
            P(None, "tensor"),
            P(None, "tensor"),
            P(("groups", "dp", "tensor"), None),
        ),
        out_specs=P(("groups", "dp", "tensor"), None),
        check_vma=False,
    )
```

```python
import jax
import jax.numpy as jnp
from jax import lax
from jax.experimental import pallas as pl
from jax.experimental.pallas import tpu as pltpu
from jax.sharding import PartitionSpec as P

K = 64
SEQ = 32
HIGHEST = lax.Precision.HIGHEST


def dot_rows(a, b):
    return lax.dot_general(a, b, (((1,), (1,)), ((), ())), preferred_element_type=jnp.float32)


def fused_kernel(
    qi_hbm, qg_hbm, fi_hbm, fo_hbm, store_hbm, out_ref,
    qi, qg, fi, fo, store, part, got, turned, spread, blocks, wide,
    load_sem, rs_send, rs_recv, ag_send, ag_recv, group_recv,
):
    depth = lax.axis_size("tensor")
    rows = qi.shape[1]
    y = lax.axis_index("groups")
    dp = lax.axis_index("dp")
    z = lax.axis_index("tensor")
    x = dp // 2
    core = dp % 2
    other_core = {"dp": x * 2 + (1 - core)}
    other_x = {"dp": (1 - x) * 2 + core}
    other_y = {"groups": 1 - y}
    other_xy = {"groups": 1 - y, "dp": (1 - x) * 2 + core}
    order = (3, 2, 1, 0)
    half = rows // 2

    def peer(step):
        return (z, z + 1 - 2 * (z % 2), lax.rem(z + 2, depth), depth - 1 - z)[step]

    def load(source, target, index):
        return pltpu.make_async_copy(source, target, load_sem.at[index])

    def chunk_loads(step):
        start = pl.multiple_of((y * depth + peer(step)) * rows, rows)
        return (
            load(qi_hbm.at[pl.ds(start, rows), :], qi.at[step], 3 + 2 * step),
            load(qg_hbm.at[pl.ds(start, rows), :], qg.at[step], 4 + 2 * step),
        )

    load(fi_hbm, fi, 0).start()
    load(fo_hbm, fo, 1).start()
    for step in order:
        for copy in chunk_loads(step):
            copy.start()
    load(store_hbm, store, 2).start()

    barrier = pltpu.get_barrier_semaphore()
    partners = [{"tensor": peer(step)} for step in range(1, 4)]
    partners += [other_core, other_x, other_y, other_xy]
    for partner in partners:
        pl.semaphore_signal(barrier, inc=1, device_id=partner, device_id_type=pl.DeviceIdType.MESH)

    def remote(source, target, send, recv, device):
        return pltpu.make_async_remote_copy(
            src_ref=source, dst_ref=target, send_sem=send, recv_sem=recv,
            device_id=device, device_id_type=pl.DeviceIdType.MESH,
        )

    def sums(kind):
        source, step = (
            (part.at[3, pl.ds(half, half)], 1),
            (part.at[3, pl.ds(0, half)], 3),
            (part.at[2, pl.ds(0, half)], 2),
            (part.at[1, pl.ds(0, half)], 1),
            (part.at[1, pl.ds(half, half)], 1),
            (part.at[2, pl.ds(half, half)], 2),
        )[kind]
        return remote(source, got.at[kind], rs_send.at[kind], rs_recv.at[kind], {"tensor": peer(step)})

    load(fi_hbm, fi, 0).wait()
    load(fo_hbm, fo, 1).wait()
    for step in order:
        for copy in chunk_loads(step):
            copy.wait()
        part[step] = jnp.concatenate([dot_rows(qi[step], fi[...]), dot_rows(qg[step], fo[...])], axis=1)
        if step == order[0]:
            pl.semaphore_wait(barrier, len(partners))
        for kind in ((), (3, 4), (2,), (0, 1))[step]:
            sums(kind).start()

    sums(0).wait_recv()
    part[2, half:] = part[2, half:] + got[0]
    sums(5).start()

    lane = lax.broadcasted_iota(jnp.int32, (half, 2 * K), 1)
    lane8 = lax.broadcasted_iota(jnp.int32, (8, 2 * half), 1)

    def query_gradients(total):
        turned[...] = jnp.concatenate([total, total], axis=0).T
        for place, pair in enumerate((0, 2, 1, 3)):
            first = turned[pl.ds(K + 2 * pair, 8, stride=8), :]
            second = turned[pl.ds(K + 2 * pair + 1, 8, stride=8), :]
            both = jnp.where(lane8 < half, first, second)
            for q in range(2):
                spread[pl.ds(place * 2 + q, 8, stride=8), :] = jnp.where((lane8 % half) // SEQ == q, both, 0.0)
        stacked = jnp.concatenate(
            [jnp.where(lane < K, total, 0.0), jnp.where(lane >= K, pltpu.roll(total, K, 1), 0.0)], axis=0
        )
        product = jnp.dot(spread[...], stacked, precision=HIGHEST, preferred_element_type=jnp.float32)
        return product.astype(jnp.bfloat16)

    def slot_of(yy, xx, zz, cc):
        return ((xx * 2 + cc) * 2 + yy) * depth + zz

    def move(part_of, slot, kind, zz, device):
        block = blocks.at[part_of * 32 + slot]
        recv = group_recv.at[part_of, slot // depth] if kind < 3 else ag_recv.at[part_of, zz]
        return remote(block, block, ag_send, recv, device)

    def four(part_of, yy, xx, cc):
        base = slot_of(yy, xx, 0, cc)
        blocks_of = blocks.at[pl.ds(part_of * 32 + base, 4)]
        return remote(blocks_of, blocks_of, ag_send, group_recv.at[part_of, base // depth], other_core)

    def column(part_of, step):
        zz = peer(step)
        slot = slot_of(y, x, zz, core)
        if step:
            move(part_of, slot, 3, zz, other_core).wait_recv()
        for kind, device in enumerate((other_xy, other_x, other_y)):
            move(part_of, slot, kind, zz, device).start()

    row8 = lax.broadcasted_iota(jnp.int32, (8, 8, 2 * K), 1)
    low = row8 < 4
    first_of_two = (row8 // 2) % 2 == 0

    def pairs(slot):
        a = blocks[slot].astype(jnp.float32).reshape(8, 8, 2 * K)
        b = blocks[32 + slot].astype(jnp.float32).reshape(8, 8, 2 * K)
        return jnp.where(first_of_two, a, pltpu.roll(b, 2, 1)), jnp.where(first_of_two, pltpu.roll(a, 6, 1), b)

    def regroup(yy, xx, cc):
        base = slot_of(yy, xx, 0, cc)
        start = pl.multiple_of(base * 4, 16)
        held = [pairs(base + zz) for zz in range(4)]
        for e in range(2):
            evens, odds = [], []
            for zz in (0, 2):
                a, b = held[zz][e], held[zz + 1][e]
                evens.append(jnp.where(low, a, pltpu.roll(b, 4, 1)))
                odds.append(jnp.where(low, pltpu.roll(a, 4, 1), b))
            even = jnp.concatenate(evens, axis=1).astype(jnp.bfloat16)
            odd = jnp.concatenate(odds, axis=1).astype(jnp.bfloat16)
            for g in range(8):
                at = (2 * g + e) * 256
                wide[pl.ds(start, 16), at : at + 128] = even[g]
                wide[pl.ds(start, 16), at + 128 : at + 256] = odd[g]

    own = slot_of(y, x, z, core)
    for part_of, kinds in ((0, (3, 1, 2)), (1, (4, 5))):
        total = part[0, part_of * half : (part_of + 1) * half]
        for kind in kinds:
            sums(kind).wait_recv()
            total = total + got[kind]
        blocks[part_of * 32 + own] = query_gradients(total)
        for step in (2, 3, 1):
            move(part_of, own, 3, z, {"tensor": peer(step)}).start()
        column(part_of, 0)

    for part_of in range(2):
        for step in (1, 3, 2):
            column(part_of, step)
        four(part_of, y, x, core).start()
    chips = ((y, x), (y, 1 - x), (1 - y, x), (1 - y, 1 - x))
    for part_of in range(2):
        for yy, xx in chips[1:]:
            four(part_of, yy, xx, core).wait_recv()
            four(part_of, yy, xx, core).start()
    for cc in (core, 1 - core):
        for yy, xx in chips:
            if cc is not core:
                for part_of in range(2):
                    four(part_of, yy, xx, cc).wait_recv()
            regroup(yy, xx, cc)

    load(store_hbm, store, 2).wait()
    out_ref[...] = dot_rows(store[...], wide[...])

    for kind in range(6):
        sums(kind).wait_send()
    every = blocks.at[pl.ds(0, 62)]
    remote(every, every, ag_send, ag_recv.at[0, z], other_core).wait_send()


def fused(query_inputs, query_grads, input_factor, output_factor, train_store):
    tokens, width = query_inputs.shape
    hidden = query_grads.shape[1]
    rows = tokens // 8
    queries = 32 * 4
    any_spec = pl.BlockSpec(memory_space=pl.ANY)
    return pl.pallas_call(
        fused_kernel,
        out_shape=jax.ShapeDtypeStruct((train_store.shape[0], queries), jnp.float32),
        in_specs=[any_spec] * 5,
        out_specs=pl.BlockSpec(memory_space=pltpu.VMEM),
        scratch_shapes=[
            pltpu.VMEM((4, rows, width), jnp.bfloat16),
            pltpu.VMEM((4, rows, hidden), jnp.bfloat16),
            pltpu.VMEM(input_factor.shape, jnp.bfloat16),
            pltpu.VMEM(output_factor.shape, jnp.bfloat16),
            pltpu.VMEM(train_store.shape, jnp.bfloat16),
            pltpu.VMEM((4, rows, 2 * K), jnp.float32),
            pltpu.VMEM((6, rows // 2, 2 * K), jnp.float32),
            pltpu.VMEM((2 * K, rows), jnp.float32),
            pltpu.VMEM((rows // 2, rows), jnp.float32),
            pltpu.VMEM((64, rows // 2, 2 * K), jnp.bfloat16),
            pltpu.VMEM((queries, K * K), jnp.bfloat16),
            pltpu.SemaphoreType.DMA((11,)),
            pltpu.SemaphoreType.DMA((6,)),
            pltpu.SemaphoreType.DMA((6,)),
            pltpu.SemaphoreType.DMA,
            pltpu.SemaphoreType.DMA((2, 4)),
            pltpu.SemaphoreType.DMA((2, 8)),
        ],
        compiler_params=pltpu.CompilerParams(
            collective_id=0, has_side_effects=True, vmem_limit_bytes=55000 * 1024
        ),
        cost_estimate=pl.CostEstimate(flops=1_000_000_000, bytes_accessed=8_000_000, transcendentals=0),
    )(query_inputs, query_grads, input_factor, output_factor, train_store)


def from_behind(value, axis, steps):
    count = lax.axis_size(axis)
    pairs = [(source, (source + steps) % count) for source in range(count)]
    return lax.ppermute(value, axis, pairs)


def outer_blocks(inputs_rows, grads_rows):
    examples = inputs_rows.shape[0] // SEQ
    blocks = jnp.einsum(
        "eto,eti->eoi",
        grads_rows.reshape(examples, SEQ, K),
        inputs_rows.reshape(examples, SEQ, K),
        precision=HIGHEST,
    )
    return blocks.reshape(examples, K * K).astype(jnp.bfloat16)


def ring(query_inputs, query_grads, input_factor, output_factor, train_store):
    inputs_part = dot_rows(query_inputs, input_factor)
    grads_part = dot_rows(query_grads, output_factor)
    inputs_full, grads_full = lax.psum((inputs_part, grads_part), "tensor")
    block = outer_blocks(inputs_full, grads_full)

    def place_block(scores, piece, start):
        return lax.dynamic_update_slice_in_dim(scores, dot_rows(train_store, piece), start, 1)

    per_owner = block.shape[0]
    cycle_size = lax.axis_size("dp")
    own_index = lax.axis_index("dp")
    scores_empty = jnp.zeros((train_store.shape[0], per_owner * cycle_size), jnp.float32)
    scores = place_block(scores_empty, block, own_index * per_owner)

    def cycle_step(turn, carry):
        held, scores = carry
        held = from_behind(held, "dp", 1)
        owner = (own_index - turn) % cycle_size
        return (held, place_block(scores, held, owner * per_owner))

    held, scores = lax.fori_loop(1, cycle_size, cycle_step, (block, scores))
    return scores


def local(query_inputs, *rest):
    sizes = tuple(lax.axis_size(axis) for axis in ("groups", "dp", "tensor"))
    if sizes == (2, 4, 4) and query_inputs.shape[0] == 8 * 4 * SEQ:
        return fused(query_inputs, *rest)
    return ring(query_inputs, *rest)


def solution(mesh):
    return jax.shard_map(
        local,
        mesh=mesh,
        in_specs=(
            P("dp", "tensor"),
            P("dp", "tensor"),
            P(None, "tensor"),
            P(None, "tensor"),
            P(("groups", "dp", "tensor"), None),
        ),
        out_specs=P(("groups", "dp", "tensor"), None),
        check_vma=False,
    )
```

```python
import jax
import jax.numpy as jnp
from jax import lax
from jax.experimental import pallas as pl
from jax.experimental.pallas import tpu as pltpu
from jax.sharding import PartitionSpec as P

K = 64
SEQ = 32
HIGHEST = lax.Precision.HIGHEST


def dot_rows(a, b):
    return lax.dot_general(a, b, (((1,), (1,)), ((), ())), preferred_element_type=jnp.float32)


def fused_kernel(
    qi_hbm, qg_hbm, fi_hbm, fo_hbm, store_hbm, out_ref,
    qi, qg, fi, fo, store, part, got, turned, spread, blocks, wide,
    load_sem, rs_send, rs_recv, ag_send, ag_recv, group_recv,
):
    depth = lax.axis_size("tensor")
    rows = qi.shape[1]
    y = lax.axis_index("groups")
    dp = lax.axis_index("dp")
    z = lax.axis_index("tensor")
    x = dp // 2
    core = dp % 2
    other_core = {"dp": x * 2 + (1 - core)}
    other_x = {"dp": (1 - x) * 2 + core}
    other_y = {"groups": 1 - y}
    other_xy = {"groups": 1 - y, "dp": (1 - x) * 2 + core}
    order = (3, 2, 1, 0)
    half = rows // 2

    def peer(step):
        return (z, z + 1 - 2 * (z % 2), lax.rem(z + 2, depth), depth - 1 - z)[step]

    def load(source, target, index):
        return pltpu.make_async_copy(source, target, load_sem.at[index])

    def chunk_loads(step):
        start = pl.multiple_of((y * depth + peer(step)) * rows, rows)
        return (
            load(qi_hbm.at[pl.ds(start, rows), :], qi.at[step], 3 + 2 * step),
            load(qg_hbm.at[pl.ds(start, rows), :], qg.at[step], 4 + 2 * step),
        )

    first_inputs, first_grads = chunk_loads(order[0])
    load(fi_hbm, fi, 0).start()
    first_inputs.start()
    load(fo_hbm, fo, 1).start()
    first_grads.start()
    for step in order[1:]:
        for copy in chunk_loads(step):
            copy.start()
    load(store_hbm, store, 2).start()

    barrier = pltpu.get_barrier_semaphore()
    partners = [{"tensor": peer(step)} for step in range(1, 4)]
    partners += [other_core, other_x, other_y, other_xy]
    for partner in partners:
        pl.semaphore_signal(barrier, inc=1, device_id=partner, device_id_type=pl.DeviceIdType.MESH)

    def remote(source, target, send, recv, device):
        return pltpu.make_async_remote_copy(
            src_ref=source, dst_ref=target, send_sem=send, recv_sem=recv,
            device_id=device, device_id_type=pl.DeviceIdType.MESH,
        )

    def sums(kind):
        source, step = (
            (part.at[3, pl.ds(half, half)], 1),
            (part.at[3, pl.ds(0, half)], 3),
            (part.at[2, pl.ds(0, half)], 2),
            (part.at[1, pl.ds(0, half)], 1),
            (part.at[1, pl.ds(half, half)], 1),
            (part.at[2, pl.ds(half, half)], 2),
        )[kind]
        return remote(source, got.at[kind], rs_send.at[kind], rs_recv.at[kind], {"tensor": peer(step)})

    load(fi_hbm, fi, 0).wait()
    for step in order:
        inputs_loaded, grads_loaded = chunk_loads(step)
        inputs_loaded.wait()
        projected_inputs = dot_rows(qi[step], fi[...])
        if step == order[0]:
            load(fo_hbm, fo, 1).wait()
        grads_loaded.wait()
        part[step] = jnp.concatenate([projected_inputs, dot_rows(qg[step], fo[...])], axis=1)
        if step == order[0]:
            pl.semaphore_wait(barrier, len(partners))
        for kind in ((), (3, 4), (2,), (0, 1))[step]:
            sums(kind).start()

    sums(0).wait_recv()
    part[2, half:] = part[2, half:] + got[0]
    sums(5).start()

    lane = lax.broadcasted_iota(jnp.int32, (half, 2 * K), 1)
    lane8 = lax.broadcasted_iota(jnp.int32, (8, 2 * half), 1)

    def query_gradients(total):
        turned[...] = jnp.concatenate([total, total], axis=0).T
        for place, pair in enumerate((0, 2, 1, 3)):
            first = turned[pl.ds(K + 2 * pair, 8, stride=8), :]
            second = turned[pl.ds(K + 2 * pair + 1, 8, stride=8), :]
            both = jnp.where(lane8 < half, first, second)
            for q in range(2):
                spread[pl.ds(place * 2 + q, 8, stride=8), :] = jnp.where((lane8 % half) // SEQ == q, both, 0.0)
        stacked = jnp.concatenate(
            [jnp.where(lane < K, total, 0.0), jnp.where(lane >= K, pltpu.roll(total, K, 1), 0.0)], axis=0
        )
        product = jnp.dot(spread[...], stacked, precision=HIGHEST, preferred_element_type=jnp.float32)
        return product.astype(jnp.bfloat16)

    def slot_of(yy, xx, zz, cc):
        return ((xx * 2 + cc) * 2 + yy) * depth + zz

    def move(part_of, slot, kind, zz, device):
        block = blocks.at[part_of * 32 + slot]
        recv = group_recv.at[part_of, slot // depth] if kind < 3 else ag_recv.at[part_of, zz]
        return remote(block, block, ag_send, recv, device)

    def four(part_of, yy, xx, cc):
        base = slot_of(yy, xx, 0, cc)
        blocks_of = blocks.at[pl.ds(part_of * 32 + base, 4)]
        return remote(blocks_of, blocks_of, ag_send, group_recv.at[part_of, base // depth], other_core)

    def column(part_of, step):
        zz = peer(step)
        slot = slot_of(y, x, zz, core)
        if step:
            move(part_of, slot, 3, zz, other_core).wait_recv()
        for kind, device in enumerate((other_xy, other_x, other_y)):
            move(part_of, slot, kind, zz, device).start()

    row8 = lax.broadcasted_iota(jnp.int32, (8, 8, 2 * K), 1)
    low = row8 < 4
    first_of_two = (row8 // 2) % 2 == 0

    def pairs(slot):
        a = blocks[slot].astype(jnp.float32).reshape(8, 8, 2 * K)
        b = blocks[32 + slot].astype(jnp.float32).reshape(8, 8, 2 * K)
        return jnp.where(first_of_two, a, pltpu.roll(b, 2, 1)), jnp.where(first_of_two, pltpu.roll(a, 6, 1), b)

    def regroup(yy, xx, cc):
        base = slot_of(yy, xx, 0, cc)
        start = pl.multiple_of(base * 4, 16)
        held = [pairs(base + zz) for zz in range(4)]
        for e in range(2):
            evens, odds = [], []
            for zz in (0, 2):
                a, b = held[zz][e], held[zz + 1][e]
                evens.append(jnp.where(low, a, pltpu.roll(b, 4, 1)))
                odds.append(jnp.where(low, pltpu.roll(a, 4, 1), b))
            even = jnp.concatenate(evens, axis=1).astype(jnp.bfloat16)
            odd = jnp.concatenate(odds, axis=1).astype(jnp.bfloat16)
            for g in range(8):
                at = (2 * g + e) * 256
                wide[pl.ds(start, 16), at : at + 128] = even[g]
                wide[pl.ds(start, 16), at + 128 : at + 256] = odd[g]

    own = slot_of(y, x, z, core)
    for part_of, kinds in ((0, (3, 1, 2)), (1, (4, 5))):
        total = part[0, part_of * half : (part_of + 1) * half]
        for kind in kinds:
            sums(kind).wait_recv()
            total = total + got[kind]
        blocks[part_of * 32 + own] = query_gradients(total)
        for step in (3, 2, 1):
            move(part_of, own, 3, z, {"tensor": peer(step)}).start()
        column(part_of, 0)

    for part_of in range(2):
        for step in (1, 2, 3):
            column(part_of, step)
        four(part_of, y, x, core).start()
    chips = ((y, x), (y, 1 - x), (1 - y, x), (1 - y, 1 - x))
    for part_of in range(2):
        for yy, xx in chips[1:]:
            four(part_of, yy, xx, core).wait_recv()
            four(part_of, yy, xx, core).start()
    for cc in (core, 1 - core):
        for yy, xx in chips:
            if cc is not core:
                for part_of in range(2):
                    four(part_of, yy, xx, cc).wait_recv()
            regroup(yy, xx, cc)

    load(store_hbm, store, 2).wait()
    out_ref[...] = dot_rows(store[...], wide[...])

    for kind in range(6):
        sums(kind).wait_send()
    every = blocks.at[pl.ds(0, 62)]
    remote(every, every, ag_send, ag_recv.at[0, z], other_core).wait_send()


def fused(query_inputs, query_grads, input_factor, output_factor, train_store):
    tokens, width = query_inputs.shape
    hidden = query_grads.shape[1]
    rows = tokens // 8
    queries = 32 * 4
    any_spec = pl.BlockSpec(memory_space=pl.ANY)
    return pl.pallas_call(
        fused_kernel,
        out_shape=jax.ShapeDtypeStruct((train_store.shape[0], queries), jnp.float32),
        in_specs=[any_spec] * 5,
        out_specs=pl.BlockSpec(memory_space=pltpu.VMEM),
        scratch_shapes=[
            pltpu.VMEM((4, rows, width), jnp.bfloat16),
            pltpu.VMEM((4, rows, hidden), jnp.bfloat16),
            pltpu.VMEM(input_factor.shape, jnp.bfloat16),
            pltpu.VMEM(output_factor.shape, jnp.bfloat16),
            pltpu.VMEM(train_store.shape, jnp.bfloat16),
            pltpu.VMEM((4, rows, 2 * K), jnp.float32),
            pltpu.VMEM((6, rows // 2, 2 * K), jnp.float32),
            pltpu.VMEM((2 * K, rows), jnp.float32),
            pltpu.VMEM((rows // 2, rows), jnp.float32),
            pltpu.VMEM((64, rows // 2, 2 * K), jnp.bfloat16),
            pltpu.VMEM((queries, K * K), jnp.bfloat16),
            pltpu.SemaphoreType.DMA((11,)),
            pltpu.SemaphoreType.DMA((6,)),
            pltpu.SemaphoreType.DMA((6,)),
            pltpu.SemaphoreType.DMA,
            pltpu.SemaphoreType.DMA((2, 4)),
            pltpu.SemaphoreType.DMA((2, 8)),
        ],
        compiler_params=pltpu.CompilerParams(
            collective_id=0, has_side_effects=True, vmem_limit_bytes=55000 * 1024
        ),
        cost_estimate=pl.CostEstimate(flops=1_000_000_000, bytes_accessed=8_000_000, transcendentals=0),
    )(query_inputs, query_grads, input_factor, output_factor, train_store)


def from_behind(value, axis, steps):
    count = lax.axis_size(axis)
    pairs = [(source, (source + steps) % count) for source in range(count)]
    return lax.ppermute(value, axis, pairs)


def outer_blocks(inputs_rows, grads_rows):
    examples = inputs_rows.shape[0] // SEQ
    blocks = jnp.einsum(
        "eto,eti->eoi",
        grads_rows.reshape(examples, SEQ, K),
        inputs_rows.reshape(examples, SEQ, K),
        precision=HIGHEST,
    )
    return blocks.reshape(examples, K * K).astype(jnp.bfloat16)


def ring(query_inputs, query_grads, input_factor, output_factor, train_store):
    inputs_part = dot_rows(query_inputs, input_factor)
    grads_part = dot_rows(query_grads, output_factor)
    inputs_full, grads_full = lax.psum((inputs_part, grads_part), "tensor")
    block = outer_blocks(inputs_full, grads_full)

    def place_block(scores, piece, start):
        return lax.dynamic_update_slice_in_dim(scores, dot_rows(train_store, piece), start, 1)

    per_owner = block.shape[0]
    cycle_size = lax.axis_size("dp")
    own_index = lax.axis_index("dp")
    scores_empty = jnp.zeros((train_store.shape[0], per_owner * cycle_size), jnp.float32)
    scores = place_block(scores_empty, block, own_index * per_owner)

    def cycle_step(turn, carry):
        held, scores = carry
        held = from_behind(held, "dp", 1)
        owner = (own_index - turn) % cycle_size
        return (held, place_block(scores, held, owner * per_owner))

    held, scores = lax.fori_loop(1, cycle_size, cycle_step, (block, scores))
    return scores


def local(query_inputs, *rest):
    sizes = tuple(lax.axis_size(axis) for axis in ("groups", "dp", "tensor"))
    if sizes == (2, 4, 4) and query_inputs.shape[0] == 8 * 4 * SEQ:
        return fused(query_inputs, *rest)
    return ring(query_inputs, *rest)


def solution(mesh):
    return jax.shard_map(
        local,
        mesh=mesh,
        in_specs=(
            P("dp", "tensor"),
            P("dp", "tensor"),
            P(None, "tensor"),
            P(None, "tensor"),
            P(("groups", "dp", "tensor"), None),
        ),
        out_specs=P(("groups", "dp", "tensor"), None),
        check_vma=False,
    )
```
